32 devices in a mesh: gx: 4 (over y, x), gy: 8 (over z, core).
Axes of the slice: x: 2, y: 2, z: 4, core: 2. Of those that a mesh axis runs over, the one named last changes fastest.
Arguments:
- f_start: float32 [19, 4, 256, 512], P(None, None, 'gy', 'gx'), may hold values from 0.022 to 0.4, as said below
- cotangent: bfloat16 [19, 4, 256, 512], P(None, None, 'gy', 'gx'), may hold values from -6 to 6
- porosity: float32 [4, 8, 16], P('gx', 'gy'), may hold values from 0.1 to 0.9
- brick_ids: int32 [4, 8, 64], P('gx', 'gy'), may hold values from 0 to 127, as said below
- brick_slot: int32 [4, 8, 64], P('gx', 'gy'), may hold values from 0 to 15
Outputs:
- start_grad: float32 [19, 4, 256, 512], P(None, None, 'gy', 'gx')
- porosity_grad: float32 [4, 8, 16], P('gx', 'gy')
The draws below stay inside these ranges and needn't reach their ends.
Inputs may be any that keep to these rules, and one draw needn't show every extreme that they name: `f_start`: each population is w_q times a factor between 0.8 and 1.2, w_q the weight of its direction. `brick_ids`: each device lists 64 distinct bricks of its own block; brick b covers layer b // 32, row b % 32 and all 128 cells along x of that block; device (0, 0) lists the last brick and device (0, 1) the first.
All inputs are finite; a program needn't handle non-finite values.
Results may differ from the reference program's by a relative error of at most 0.0003.
Values sent between devices are 32-bit elements; how exact they have to be, the bound alone decides.
A program may use at most 64 MiB of HBM per device.

```python
import jax
import jax.numpy as jnp
import numpy as np
from jax import lax

Z = 4
CX = 128
CY = 32
NB = 64
SLOTS = 16
NX = 512
NY = 256
N_GX = 4
N_GY = 8


WEIGHT_TABLE = np.array([1.0 / 3.0] + [1.0 / 18.0] * 6 + [1.0 / 36.0] * 12, dtype=np.float32)


def draw_f_start(key, part):
    shape = (19, Z, NY, NX)
    weights = jnp.asarray(WEIGHT_TABLE)[:, None, None, None]
    factor = jax.random.uniform(key, shape, jnp.float32, 0.8, 1.2)
    return weights * factor


def draw_brick_ids(key, part):
    brick_count = Z * CY * (CX // 128)
    device_count = N_GX * N_GY
    key_list = jax.random.split(key, device_count)
    orders = jax.vmap(lambda single: jax.random.permutation(single, brick_count))(key_list)
    device_row = jnp.arange(device_count, dtype=jnp.int32)[:, None]
    leading = orders[:, :1]
    to_last = (orders + (brick_count - 1 - leading)) % brick_count
    to_first = (orders - leading) % brick_count
    orders = jnp.where(device_row == 0, to_last, jnp.where(device_row == 1, to_first, orders))
    return orders[:, :NB].reshape(N_GX, N_GY, NB).astype(jnp.int32)


def place_ends(values, stream_key, low, high):
    longest = values.shape.index(max(values.shape))
    spots = []
    for shift in (0, 1):
        where = [jax.random.randint(jax.random.fold_in(stream_key, axis), (), 0, length) for axis, length in enumerate(values.shape)]
        where[longest] = (where[longest] + shift) % values.shape[longest]
        spots.append(tuple(where))
    return values.at[spots[0]].set(low).at[spots[1]].set(high)


def block_levels(stream_key, extent, cuts, smallest, largest):
    factor_of, own = 1.0, jax.random.fold_in(stream_key, 6)
    for axis_at, parts in cuts:
        draws = jnp.exp(jax.random.uniform(jax.random.fold_in(own, axis_at), (parts,), jnp.float32, smallest / len(cuts), largest / len(cuts)))
        factor_of = factor_of * jnp.repeat(draws, extent[axis_at] // parts).reshape([-1 if axis == axis_at else 1 for axis in range(len(extent))])
    return factor_of


def noise(rng, shape, scale, limit, cuts=(), held_as=jnp.bfloat16):
    gain = block_levels(rng, shape, cuts, -0.22, 0.18) if cuts else 1.0
    drawn = jax.random.normal(rng, shape, jnp.float32) * scale * gain
    return jnp.minimum(jnp.maximum(drawn, -limit), limit).astype(held_as)


def setup_inputs(seed: int = 0) -> dict:
    arg_keys = jax.random.split(jax.random.key(seed), 6)
    f_start = draw_f_start(jax.random.fold_in(arg_keys[5], 71), 0)
    cotangent = noise(arg_keys[1], (19, Z, NY, NX), 1.0, 6.0, ((2, 8), (3, 4)))
    porosity = jnp.clip(0.1 + 0.79999997 * jax.random.uniform(arg_keys[2], (N_GX, N_GY, SLOTS), jnp.float32) ** block_levels(arg_keys[2], (N_GX, N_GY, SLOTS), ((0, 4), (1, 8)), -0.2, 0.2), 0.1, 0.9)
    brick_ids = draw_brick_ids(jax.random.fold_in(arg_keys[5], 71), 0)
    brick_slot = place_ends(jax.random.randint(arg_keys[4], (N_GX, N_GY, NB), 0, SLOTS), jax.random.fold_in(arg_keys[4], 1), 0, SLOTS - 1).astype(jnp.int32)
    return {"f_start": f_start, "cotangent": cotangent, "porosity": porosity, "brick_ids": brick_ids, "brick_slot": brick_slot}


DIR_X = np.array([0, 1, -1, 0, 0, 0, 0, 1, -1, 1, -1, 1, -1, 1, -1, 0, 0, 0, 0])
DIR_Y = np.array([0, 0, 0, 1, -1, 0, 0, 1, 1, -1, -1, 0, 0, 0, 0, 1, -1, 1, -1])
DIR_Z = np.array([0, 0, 0, 0, 0, 1, -1, 0, 0, 0, 0, 1, 1, -1, -1, 1, 1, -1, -1])
WEIGHTS = np.array([1.0 / 3.0] + [1.0 / 18.0] * 6 + [1.0 / 36.0] * 12)
RELAX_RATE = 0.8

def column(values):
    return np.asarray(values, np.float32)[:, None, None, None]

def collide(field, solid):
    density = lax.optimization_barrier(jnp.sum(field, axis=0))
    inverse = (1.0 - solid) / density
    vel_x = lax.optimization_barrier(jnp.sum(field * column(DIR_X), axis=0)) * inverse
    vel_y = lax.optimization_barrier(jnp.sum(field * column(DIR_Y), axis=0)) * inverse
    vel_z = lax.optimization_barrier(jnp.sum(field * column(DIR_Z), axis=0)) * inverse
    along = column(DIR_X) * vel_x + column(DIR_Y) * vel_y + column(DIR_Z) * vel_z
    square = vel_x * vel_x + vel_y * vel_y + vel_z * vel_z
    balance = column(WEIGHTS) * density * (1.0 + 3.0 * along + 4.5 * along * along - 1.5 * square)
    return field - RELAX_RATE * (field - balance)

def collide_layers(field, solid):
    moved = jnp.moveaxis(field, 1, 0)
    result = lax.map(lambda pair: collide(pair[0][:, None], pair[1][None])[:, 0], (moved, solid))
    return jnp.moveaxis(result, 0, 1)

def collide_back(field, solid, incoming):

    def one_layer(items):
        layer, solid_layer, cot_layer = items
        ignored, undo_layer = jax.vjp(collide, layer[:, None], solid_layer[None])
        grad_field, grad_solid = undo_layer(cot_layer[:, None])
        return (grad_field[:, 0], grad_solid[0])
    grad_field, grad_solid = lax.map(one_layer, (jnp.moveaxis(field, 1, 0), solid, jnp.moveaxis(incoming, 1, 0)))
    return (jnp.moveaxis(grad_field, 0, 1), grad_solid)

def stream(field, sign):
    moved = []
    for lane in range(19):
        offset = (sign * int(DIR_Z[lane]), sign * int(DIR_Y[lane]), sign * int(DIR_X[lane]))
        moved.append(jnp.roll(field[lane], offset, axis=(0, 1, 2)))
    return jnp.stack(moved)

def reference(f_start, cotangent, porosity, brick_ids, brick_slot):
    tile_count = CX // 128
    brick_count = Z * CY * tile_count
    brick_hit = (brick_ids[..., None] == jnp.arange(brick_count, dtype=jnp.int32)).astype(jnp.float32)
    slot_hit = (brick_slot[..., None] == jnp.arange(SLOTS, dtype=jnp.int32)).astype(jnp.float32)
    brick_value = lax.optimization_barrier(jnp.sum(slot_hit * porosity[:, :, None, :], axis=3))
    tile_value = lax.optimization_barrier(jnp.sum(brick_hit * brick_value[..., None], axis=2))
    grid_tiles = tile_value.reshape(N_GX, N_GY, Z, CY, tile_count).transpose(2, 1, 3, 0, 4).reshape(Z, NY, NX // 128)
    solid = jnp.broadcast_to(grid_tiles[..., None], (Z, NY, NX // 128, 128)).reshape(Z, NY, NX)
    after_one = stream(collide_layers(f_start, solid), 1)
    back_two = stream(cotangent.astype(jnp.float32), -1)
    back_one, solid_bar_two = collide_back(after_one, solid, back_two)
    start_grad, solid_bar_one = collide_back(f_start, solid, stream(back_one, -1))
    solid_bar = solid_bar_one + solid_bar_two
    tile_sums = solid_bar.reshape(Z, N_GY, CY, N_GX, tile_count, 128).sum(axis=5)
    tile_sums = tile_sums.transpose(3, 1, 0, 2, 4).reshape(N_GX, N_GY, brick_count)
    brick_sum = lax.optimization_barrier(jnp.sum(brick_hit * tile_sums[:, :, None, :], axis=3))
    porosity_grad = lax.optimization_barrier(jnp.sum(slot_hit * brick_sum[..., None], axis=2))
    return (start_grad, porosity_grad)
```

```python
import functools

import jax
import jax.numpy as jnp
from jax import lax
from jax.experimental import pallas as pl
from jax.experimental.pallas import tpu as pltpu
from jax.sharding import PartitionSpec as P

EX = (0, 1, -1, 0, 0, 0, 0, 1, -1, 1, -1, 1, -1, 1, -1, 0, 0, 0, 0)
EY = (0, 0, 0, 1, -1, 0, 0, 1, 1, -1, -1, 0, 0, 0, 0, 1, -1, 1, -1)
EZ = (0, 0, 0, 0, 0, 1, -1, 0, 0, 0, 0, 1, 1, -1, -1, 1, 1, -1, -1)
Q = 19
PAIRS = ((1, 2), (3, 4), (5, 6), (7, 10), (9, 8), (11, 14), (13, 12), (15, 18), (17, 16))
AXIS_W = 1.0 / 18.0
EDGE_W = 1.0 / 36.0
MESH = pl.DeviceIdType.MESH


def rank_among(q, component):
    return [p for p in range(Q) if component[p] == component[q]].index(q)


def side(step):
    return 0 if step > 0 else 1


def moments(d):
    return (
        (d[0], d[3] + d[4] + d[5] + d[6]),
        (d[1], (d[3] - d[4]) + (d[7] + d[8])),
        (d[2], (d[5] - d[6]) + (d[7] - d[8])),
    )


def along(vec):
    x, y, z = vec
    return (x, y, z, x + y, x - y, x + z, x - z, y + z, y - z)


def density_velocity(f, s):
    rho = f[0]
    diffs = []
    for a, b in PAIRS:
        rho = rho + (f[a] + f[b])
        diffs.append(f[a] - f[b])
    m = [a + b for a, b in moments(diffs)]
    inverse = s / rho
    return rho, m, [c * inverse for c in m]


def collide(f, rho, v):
    square = v[0] * v[0] + v[1] * v[1] + v[2] * v[2]
    base = 1.0 - 1.5 * square
    out = [None] * Q
    rho_axis = (0.8 * AXIS_W) * rho
    rho_edge = (0.8 * EDGE_W) * rho
    out[0] = 0.2 * f[0] + (0.8 / 3.0) * rho * base
    for n, ((a, b), c) in enumerate(zip(PAIRS, along(v))):
        scale = rho_axis if n < 3 else rho_edge
        even = scale * (base + 4.5 * c * c)
        odd = scale * (3.0 * c)
        out[a] = 0.2 * f[a] + (even + odd)
        out[b] = 0.2 * f[b] + (even - odd)
    return out


def collide_back(g, m, v, s):
    p = [g[a] + g[b] for a, b in PAIRS]
    d = [g[a] - g[b] for a, b in PAIRS]
    g1 = [AXIS_W * a + EDGE_W * b for a, b in moments(d)]
    xy, xz, yz = p[3] + p[4], p[5] + p[6], p[7] + p[8]
    g0 = (1.0 / 3.0) * g[0] + AXIS_W * (p[0] + p[1] + p[2]) + EDGE_W * (xy + xz + yz)
    gxx = AXIS_W * p[0] + EDGE_W * (xy + xz)
    gyy = AXIS_W * p[1] + EDGE_W * (xy + yz)
    gzz = AXIS_W * p[2] + EDGE_W * (xz + yz)
    gxy = EDGE_W * (p[3] - p[4])
    gxz = EDGE_W * (p[5] - p[6])
    gyz = EDGE_W * (p[7] - p[8])
    h = (
        gxx * v[0] + gxy * v[1] + gxz * v[2],
        gxy * v[0] + gyy * v[1] + gyz * v[2],
        gxz * v[0] + gyz * v[1] + gzz * v[2],
    )
    square = v[0] * v[0] + v[1] * v[1] + v[2] * v[2]
    b = [3.0 * g1[i] + 9.0 * h[i] - 3.0 * (g0 * v[i]) for i in range(3)]
    rest = g0 * (1.0 + 1.5 * square) - 4.5 * (v[0] * h[0] + v[1] * h[1] + v[2] * h[2])
    base = 0.8 * rest
    scale = 0.8 * s
    out = [None] * Q
    out[0] = 0.2 * g[0] + base
    for (a, o), c in zip(PAIRS, along([scale * c for c in b])):
        out[a] = 0.2 * g[a] + (base + c)
        out[o] = 0.2 * g[o] + (base - c)
    solid_bar = -0.8 * (b[0] * m[0] + b[1] * m[1] + b[2] * m[2])
    return out, solid_bar


def kernel(
    f_ref, cot_ref, por_ref, ids_ref, slot_ref, grad_ref, pgrad_ref,
    s_ref, v_ref, m_ref, sb_ref, a_ref, b_ref, c_ref,
    xs1, xr1, ys1, yr1, cs1, cr1, xs2, xr2, ys2, yr2, cs2, cr2, send_sem, recv_sem,
):
    layers, rows, cols = f_ref.shape[1:]
    n_x, n_y = lax.axis_size("gx"), lax.axis_size("gy")
    my_x, my_y = lax.axis_index("gx"), lax.axis_index("gy")

    def device(dx, dy):
        return (lax.rem(my_x + dx + n_x, n_x), lax.rem(my_y + dy + n_y, n_y))

    straight = ((1, 0), (-1, 0), (0, 1), (0, -1))
    corners = ((1, 1), (1, -1), (-1, 1), (-1, -1))
    barrier = pltpu.get_barrier_semaphore()
    for dx, dy in straight + corners:
        pl.semaphore_signal(barrier, inc=1, device_id=device(dx, dy), device_id_type=MESH)

    lane = lax.broadcasted_iota(jnp.int32, (rows, cols), 1)
    row = lax.broadcasted_iota(jnp.int32, (rows, cols), 0)
    lane1 = lax.broadcasted_iota(jnp.int32, (1, cols), 1)

    def copies(phase, xs, xr, ys, yr, cs, cr):
        out = []
        for n, (dx, dy) in enumerate(straight + corners):
            if n < 2:
                src, dst = xs.at[n], xr.at[n]
            elif n < 4:
                src, dst = ys.at[n - 2], yr.at[n - 2]
            else:
                src, dst = cs.at[n - 4], cr.at[n - 4]
            out.append(
                pltpu.make_async_remote_copy(
                    src_ref=src, dst_ref=dst,
                    send_sem=send_sem.at[phase, n], recv_sem=recv_sem.at[phase, n],
                    device_id=device(dx, dy), device_id_type=MESH,
                )
            )
        return out

    def pack(parts, xs, ys, cs):
        def layer(z, carry):
            carry = list(carry)
            for kind, (read, sign) in enumerate(parts):
                for q in range(Q):
                    dx, dy = sign * EX[q], sign * EY[q]
                    if not dx and not dy:
                        continue
                    plane = read(q, z)
                    if dx:
                        j = kind * 5 * layers + rank_among(q, EX) * layers + z
                        start = cols - 1 if dx > 0 else 0
                        moved = pltpu.roll(plane, lax.rem(j - start + cols, cols), 1)
                        carry[side(dx)] = jnp.where(lane == j, moved, carry[side(dx)])
                    if dy:
                        jy = kind * 5 * layers + rank_among(q, EY) * layers + z
                        edge = plane[rows - 8 :] if dy > 0 else plane[:8]
                        if dx:
                            edge = pltpu.roll(edge, dx % cols, 1)
                        edge = edge[7:8] if dy > 0 else edge[0:1]
                        ys[side(dy), pl.ds(jy, 1), :] = edge
                        if dx:
                            cs[2 * side(dx) + side(dy), pl.ds(kind * layers + z, 1), :] = edge
            return tuple(carry)

        zero = jnp.zeros((rows, cols), jnp.float32)
        ends = lax.fori_loop(0, layers, layer, (zero, zero))
        xs[0] = ends[0]
        xs[1] = ends[1]

    def stream(read, sign, kind, xr, yr, cr, write):
        def layer(z, carry):
            for q in range(Q):
                dx, dy, dz = sign * EX[q], sign * EY[q], sign * EZ[q]
                from_z = lax.rem(z - dz + layers, layers) if dz else z
                plane = read(q, from_z)
                end = 0 if dx > 0 else cols - 1
                if dx:
                    plane = pltpu.roll(plane, dx % cols, 1)
                    j = kind * 5 * layers + rank_among(q, EX) * layers + from_z
                    column = pltpu.roll(xr[side(dx)], lax.rem(end - j + cols, cols), 1)
                    plane = jnp.where(lane == end, column, plane)
                if dy:
                    plane = pltpu.roll(plane, dy % rows, 0)
                    jy = kind * 5 * layers + rank_among(q, EY) * layers + from_z
                    edge = yr[side(dy), pl.ds(jy, 1), :]
                    if dx:
                        corner = cr[2 * side(dx) + side(dy), pl.ds(kind * layers + from_z, 1), :]
                        edge = jnp.where(lane1 == end, corner, edge)
                    plane = jnp.where(row == (0 if dy > 0 else rows - 1), edge, plane)
                write(q, z, plane)
            return carry

        lax.fori_loop(0, layers, layer, 0)

    bricks = layers * rows
    ids = ids_ref[0]
    slots = slot_ref[0]
    listed = ids.shape[1]
    value = jnp.zeros((1, listed), jnp.float32)
    for k in range(por_ref.shape[2]):
        value = jnp.where(slots == k, por_ref[0, 0, k], value)
    brick_of_row = lax.broadcasted_iota(jnp.int32, (bricks, listed), 0)
    hit = brick_of_row == ids
    solid = jnp.sum(jnp.where(hit, value, 0.0), axis=1, keepdims=True)
    s_ref[...] = jnp.broadcast_to(1.0 - solid, (bricks, cols)).reshape(layers, rows, cols)

    chunks = rows // 8

    def each_chunk(body):
        def step(i, carry):
            z = lax.div(i, chunks)
            r = pl.multiple_of(lax.rem(i, chunks) * 8, 8)
            body(z, pl.ds(r, 8))
            return carry

        lax.fori_loop(0, layers * chunks, step, 0)

    def first_collision(z, r):
        f = [f_ref[q, z, r, :] for q in range(Q)]
        rho, m, v = density_velocity(f, s_ref[z, r, :])
        for i in range(3):
            v_ref[i, z, r, :] = v[i]
            m_ref[i, z, r, :] = m[i]
        for q, value in enumerate(collide(f, rho, v)):
            c_ref[q, z, r, :] = value

    each_chunk(first_collision)

    def read_c(q, z):
        return c_ref[q, z]

    def read_cot(q, z):
        return cot_ref[q, z].astype(jnp.float32)

    pack(((read_c, 1), (read_cot, -1)), xs1, ys1, cs1)
    pl.semaphore_wait(barrier, len(straight + corners))
    first = copies(0, xs1, xr1, ys1, yr1, cs1, cr1)
    for copy in first:
        copy.start()
    for copy in first:
        copy.wait()

    def write_a(q, z, plane):
        a_ref[q, z] = plane

    def write_b(q, z, plane):
        b_ref[q, z] = plane

    stream(read_c, 1, 0, xr1, yr1, cr1, write_a)
    stream(read_cot, -1, 1, xr1, yr1, cr1, write_b)

    def second_back(z, r):
        s = s_ref[z, r, :]
        rho, m, v = density_velocity([a_ref[q, z, r, :] for q in range(Q)], s)
        back, bar = collide_back([b_ref[q, z, r, :] for q in range(Q)], m, v, s)
        sb_ref[z, r, :] = bar
        for q, value in enumerate(back):
            c_ref[q, z, r, :] = value

    each_chunk(second_back)

    pack(((read_c, -1),), xs2, ys2, cs2)
    second = copies(1, xs2, xr2, ys2, yr2, cs2, cr2)
    for copy in second:
        copy.start()
    for copy in second:
        copy.wait()
    stream(read_c, -1, 0, xr2, yr2, cr2, write_a)

    def first_back(z, r):
        v = [v_ref[i, z, r, :] for i in range(3)]
        m = [m_ref[i, z, r, :] for i in range(3)]
        back, bar = collide_back([a_ref[q, z, r, :] for q in range(Q)], m, v, s_ref[z, r, :])
        sb_ref[z, r, :] = sb_ref[z, r, :] + bar
        for q, value in enumerate(back):
            grad_ref[q, z, r, :] = value

    each_chunk(first_back)

    sums = jnp.sum(sb_ref[...].reshape(bricks, cols), axis=1, keepdims=True)
    brick_sum = jnp.sum(jnp.where(hit, sums, 0.0), axis=0, keepdims=True)
    table = por_ref.shape[2]
    slot_of_row = lax.broadcasted_iota(jnp.int32, (table, listed), 0)
    slot_sum = jnp.sum(jnp.where(slot_of_row == slots, brick_sum, 0.0), axis=1, keepdims=True)
    diagonal = lax.broadcasted_iota(jnp.int32, (table, table), 0) == lax.broadcasted_iota(
        jnp.int32, (table, table), 1
    )
    pgrad_ref[0] = jnp.sum(jnp.where(diagonal, slot_sum, 0.0), axis=0, keepdims=True)


def on_device(f_start, cotangent, porosity, brick_ids, brick_slot):
    _, layers, rows, cols = f_start.shape
    vmem = pl.BlockSpec(memory_space=pltpu.VMEM)
    field = pltpu.VMEM((Q, layers, rows, cols), jnp.float32)
    vector = pltpu.VMEM((3, layers, rows, cols), jnp.float32)
    scalar = pltpu.VMEM((layers, rows, cols), jnp.float32)

    def up8(count):
        return -(-count // 8) * 8

    halos = []
    for kinds in (2, 1):
        x = pltpu.VMEM((2, rows, cols), jnp.float32)
        y = pltpu.VMEM((2, up8(kinds * 5 * layers), cols), jnp.float32)
        c = pltpu.VMEM((4, up8(kinds * layers), cols), jnp.float32)
        halos += [x, x, y, y, c, c]
    return pl.pallas_call(
        kernel,
        out_shape=(
            jax.ShapeDtypeStruct(f_start.shape, jnp.float32),
            jax.ShapeDtypeStruct(porosity.shape, jnp.float32),
        ),
        in_specs=[vmem, vmem, pl.BlockSpec(memory_space=pltpu.SMEM), vmem, vmem],
        out_specs=(vmem, vmem),
        scratch_shapes=[scalar, vector, vector, scalar, field, field, field]
        + halos
        + [pltpu.SemaphoreType.DMA((2, 8)), pltpu.SemaphoreType.DMA((2, 8))],
        compiler_params=pltpu.CompilerParams(
            collective_id=0, has_side_effects=True, vmem_limit_bytes=40 * 1024 * 1024
        ),
    )(f_start, cotangent, porosity, brick_ids, brick_slot)


def solution(mesh):
    field = P(None, None, "gy", "gx")
    table = P("gx", "gy", None)
    return jax.shard_map(
        on_device,
        mesh=mesh,
        in_specs=(field, field, table, table, table),
        out_specs=(field, table),
        check_vma=False,
    )
```

```python
import jax
import jax.numpy as jnp
from jax import lax
from jax.experimental import pallas as pl
from jax.experimental.pallas import tpu as pltpu
from jax.sharding import PartitionSpec as P

EX = (0, 1, -1, 0, 0, 0, 0, 1, -1, 1, -1, 1, -1, 1, -1, 0, 0, 0, 0)
EY = (0, 0, 0, 1, -1, 0, 0, 1, 1, -1, -1, 0, 0, 0, 0, 1, -1, 1, -1)
EZ = (0, 0, 0, 0, 0, 1, -1, 0, 0, 0, 0, 1, 1, -1, -1, 1, 1, -1, -1)
Q = 19
PAIRS = ((1, 2), (3, 4), (5, 6), (7, 10), (9, 8), (11, 14), (13, 12), (15, 18), (17, 16))
AXIS_W = 1.0 / 18.0
EDGE_W = 1.0 / 36.0
MESH = pl.DeviceIdType.MESH


def rank_among(q, component):
    return [p for p in range(Q) if component[p] == component[q]].index(q)


def side(step):
    return 0 if step > 0 else 1


def moments(d):
    return (
        (d[0], d[3] + d[4] + d[5] + d[6]),
        (d[1], (d[3] - d[4]) + (d[7] + d[8])),
        (d[2], (d[5] - d[6]) + (d[7] - d[8])),
    )


def along(vec):
    x, y, z = vec
    return (x, y, z, x + y, x - y, x + z, x - z, y + z, y - z)


def density_velocity(f, s):
    rho = f[0]
    diffs = []
    for a, b in PAIRS:
        rho = rho + (f[a] + f[b])
        diffs.append(f[a] - f[b])
    m = [a + b for a, b in moments(diffs)]
    inverse = s / rho
    return rho, m, [c * inverse for c in m]


def collide(f, rho, v):
    square = v[0] * v[0] + v[1] * v[1] + v[2] * v[2]
    base = 1.0 - 1.5 * square
    out = [None] * Q
    rho_axis = (0.8 * AXIS_W) * rho
    rho_edge = (0.8 * EDGE_W) * rho
    out[0] = 0.2 * f[0] + (0.8 / 3.0) * rho * base
    for n, ((a, b), c) in enumerate(zip(PAIRS, along(v))):
        scale = rho_axis if n < 3 else rho_edge
        even = scale * (base + 4.5 * c * c)
        odd = scale * (3.0 * c)
        out[a] = 0.2 * f[a] + (even + odd)
        out[b] = 0.2 * f[b] + (even - odd)
    return out


def collide_back(g, m, v, s):
    p = [g[a] + g[b] for a, b in PAIRS]
    d = [g[a] - g[b] for a, b in PAIRS]
    g1 = [AXIS_W * a + EDGE_W * b for a, b in moments(d)]
    xy, xz, yz = p[3] + p[4], p[5] + p[6], p[7] + p[8]
    g0 = (1.0 / 3.0) * g[0] + AXIS_W * (p[0] + p[1] + p[2]) + EDGE_W * (xy + xz + yz)
    gxx = AXIS_W * p[0] + EDGE_W * (xy + xz)
    gyy = AXIS_W * p[1] + EDGE_W * (xy + yz)
    gzz = AXIS_W * p[2] + EDGE_W * (xz + yz)
    gxy = EDGE_W * (p[3] - p[4])
    gxz = EDGE_W * (p[5] - p[6])
    gyz = EDGE_W * (p[7] - p[8])
    h = (
        gxx * v[0] + gxy * v[1] + gxz * v[2],
        gxy * v[0] + gyy * v[1] + gyz * v[2],
        gxz * v[0] + gyz * v[1] + gzz * v[2],
    )
    square = v[0] * v[0] + v[1] * v[1] + v[2] * v[2]
    b = [3.0 * g1[i] + 9.0 * h[i] - 3.0 * (g0 * v[i]) for i in range(3)]
    rest = g0 * (1.0 + 1.5 * square) - 4.5 * (v[0] * h[0] + v[1] * h[1] + v[2] * h[2])
    base = 0.8 * rest
    scale = 0.8 * s
    out = [None] * Q
    out[0] = 0.2 * g[0] + base
    for (a, o), c in zip(PAIRS, along([scale * c for c in b])):
        out[a] = 0.2 * g[a] + (base + c)
        out[o] = 0.2 * g[o] + (base - c)
    solid_bar = -0.8 * (b[0] * m[0] + b[1] * m[1] + b[2] * m[2])
    return out, solid_bar


def each_chunk(layers, rows, step_rows, body, first=0):
    chunks = rows // step_rows

    def step(i, carry):
        body(first + lax.div(i, chunks), pl.ds(pl.multiple_of(lax.rem(i, chunks) * step_rows, step_rows), step_rows))
        return carry

    lax.fori_loop(0, layers * chunks, step, 0)


def forward_kernel(
    f_hbm, cot_hbm, por_hbm, ids_hbm, slot_hbm,
    a_ref, s_ref, v_ref, m_ref, sb_ref, ids_ref, slot_ref,
    f_ref, cot_ref, por_ref, b_ref, c_ref,
    xs1, xr1, ys1, yr1, cs1, cr1, xs2, xr2, ys2, yr2, cs2, cr2, load_sem, layer_sem, send_sem, recv_sem,
):
    layers, rows, cols = f_ref.shape[1:]
    n_x, n_y = lax.axis_size("gx"), lax.axis_size("gy")
    my_x, my_y = lax.axis_index("gx"), lax.axis_index("gy")

    def device(dx, dy):
        return (lax.rem(my_x + dx + n_x, n_x), lax.rem(my_y + dy + n_y, n_y))

    straight = ((1, 0), (-1, 0), (0, 1), (0, -1))
    corners = ((1, 1), (1, -1), (-1, 1), (-1, -1))
    barrier = pltpu.get_barrier_semaphore()
    loads = [
        pltpu.make_async_copy(src, dst, load_sem.at[n])
        for n, (src, dst) in enumerate(
            ((por_hbm, por_ref), (ids_hbm, ids_ref), (slot_hbm, slot_ref), (cot_hbm, cot_ref))
        )
    ]
    layer_loads = [
        pltpu.make_async_copy(f_hbm.at[:, z], f_ref.at[:, z], layer_sem.at[z]) for z in range(layers)
    ]
    for copy in loads + layer_loads:
        copy.start()
    for dx, dy in straight + corners:
        pl.semaphore_signal(barrier, inc=1, device_id=device(dx, dy), device_id_type=MESH)

    lane = lax.broadcasted_iota(jnp.int32, (rows, cols), 1)
    lane1 = lax.broadcasted_iota(jnp.int32, (1, cols), 1)

    def copies(phase, xs, xr, ys, yr, cs, cr):
        out = []
        for n, (dx, dy) in enumerate(straight + corners):
            if n < 2:
                src, dst = xs.at[n], xr.at[n]
            elif n < 4:
                src, dst = ys.at[n - 2], yr.at[n - 2]
            else:
                src, dst = cs.at[n - 4], cr.at[n - 4]
            out.append(
                pltpu.make_async_remote_copy(
                    src_ref=src, dst_ref=dst,
                    send_sem=send_sem.at[phase, n], recv_sem=recv_sem.at[phase, n],
                    device_id=device(dx, dy), device_id_type=MESH,
                )
            )
        return out

    def pack(read, sign, kind, ys, cs, carry):
        def layer(z, carry):
            carry = list(carry)
            for q in range(Q):
                dx, dy = sign * EX[q], sign * EY[q]
                if not dx and not dy:
                    continue
                plane = read(q, z)
                if dx:
                    j = kind * 5 * layers + rank_among(q, EX) * layers + z
                    start = cols - 1 if dx > 0 else 0
                    moved = pltpu.roll(plane, lax.rem(j - start + cols, cols), 1)
                    carry[side(dx)] = jnp.where(lane == j, moved, carry[side(dx)])
                if dy:
                    jy = kind * 5 * layers + rank_among(q, EY) * layers + z
                    edge = plane[rows - 8 :] if dy > 0 else plane[:8]
                    if dx:
                        edge = pltpu.roll(edge, dx % cols, 1)
                    edge = edge[7:8] if dy > 0 else edge[0:1]
                    ys[side(dy), pl.ds(jy, 1), :] = edge
                    if dx:
                        cs[2 * side(dx) + side(dy), pl.ds(kind * layers + z, 1), :] = edge
            return tuple(carry)

        return lax.fori_loop(0, layers, layer, carry)

    def stream(read, sign, out):
        def layer(z, carry):
            for q in range(Q):
                dx, dy, dz = sign * EX[q], sign * EY[q], sign * EZ[q]
                plane = read(q, lax.rem(z - dz + layers, layers) if dz else z)
                if dx:
                    plane = pltpu.roll(plane, dx % cols, 1)
                if dy:
                    plane = pltpu.roll(plane, dy % rows, 0)
                out[q, z] = plane
            return carry

        lax.fori_loop(0, layers, layer, 0)

    def edges(sign, kind, xr, yr, cr, out):
        def layer(z, carry):
            for q in range(Q):
                dx, dy, dz = sign * EX[q], sign * EY[q], sign * EZ[q]
                if not dx and not dy:
                    continue
                from_z = lax.rem(z - dz + layers, layers) if dz else z
                end = 0 if dx > 0 else cols - 1
                if dx:
                    j = kind * 5 * layers + rank_among(q, EX) * layers + from_z
                    column = pltpu.roll(xr[side(dx)], lax.rem(end - j + cols, cols), 1)
                    if dy:
                        column = pltpu.roll(column, dy % rows, 0)
                    out[q, z] = jnp.where(lane == end, column, out[q, z])
                if dy:
                    jy = kind * 5 * layers + rank_among(q, EY) * layers + from_z
                    edge = yr[side(dy), pl.ds(jy, 1), :]
                    if dx:
                        corner = cr[2 * side(dx) + side(dy), pl.ds(kind * layers + from_z, 1), :]
                        edge = jnp.where(lane1 == end, corner, edge)
                    at = 0 if dy > 0 else rows - 1
                    out[q, z, at : at + 1, :] = edge
            return carry

        lax.fori_loop(0, layers, layer, 0)

    for copy in loads[:3]:
        copy.wait()
    bricks = layers * rows
    ids = ids_ref[0]
    slots = slot_ref[0]
    listed = ids.shape[1]
    value = jnp.zeros((1, listed), jnp.float32)
    for k in range(por_ref.shape[2]):
        value = jnp.where(slots == k, por_ref[0, 0, k], value)
    hit = lax.broadcasted_iota(jnp.int32, (bricks, listed), 0) == ids
    solid = jnp.sum(jnp.where(hit, value, 0.0), axis=1, keepdims=True)
    s_ref[...] = jnp.broadcast_to(1.0 - solid, (bricks, cols)).reshape(layers, rows, cols)

    def read_c(q, z):
        return c_ref[q, z]

    def read_cot(q, z):
        return cot_ref[q, z].astype(jnp.float32)

    zero = jnp.zeros((rows, cols), jnp.float32)
    loads[3].wait()
    ends = pack(read_cot, -1, 1, ys1, cs1, (zero, zero))

    def first_collision(z, r):
        f = [f_ref[q, z, r, :] for q in range(Q)]
        rho, m, v = density_velocity(f, s_ref[z, r, :])
        for i in range(3):
            v_ref[i, z, r, :] = v[i]
            m_ref[i, z, r, :] = m[i]
        for q, value in enumerate(collide(f, rho, v)):
            c_ref[q, z, r, :] = value

    for z in range(layers):
        layer_loads[z].wait()
        each_chunk(1, rows, 16, first_collision, z)

    ends = pack(read_c, 1, 0, ys1, cs1, ends)
    xs1[0] = ends[0]
    xs1[1] = ends[1]
    pl.semaphore_wait(barrier, len(straight + corners))
    first = copies(0, xs1, xr1, ys1, yr1, cs1, cr1)
    for copy in first:
        copy.start()
    stream(read_c, 1, a_ref)
    stream(read_cot, -1, b_ref)
    for copy in first:
        copy.wait()
    edges(1, 0, xr1, yr1, cr1, a_ref)
    edges(-1, 1, xr1, yr1, cr1, b_ref)

    def second_back(z, r):
        s = s_ref[z, r, :]
        rho, m, v = density_velocity([a_ref[q, z, r, :] for q in range(Q)], s)
        back, bar = collide_back([b_ref[q, z, r, :] for q in range(Q)], m, v, s)
        sb_ref[z, r, :] = bar
        for q, value in enumerate(back):
            c_ref[q, z, r, :] = value

    each_chunk(layers, rows, 16, second_back)

    ends = pack(read_c, -1, 0, ys2, cs2, (zero, zero))
    xs2[0] = ends[0]
    xs2[1] = ends[1]
    second = copies(1, xs2, xr2, ys2, yr2, cs2, cr2)
    for copy in second:
        copy.start()
    stream(read_c, -1, a_ref)
    for copy in second:
        copy.wait()
    edges(-1, 0, xr2, yr2, cr2, a_ref)


def last_kernel(
    g_ref, s_ref, v_ref, m_ref, sb_ref, ids_ref, slot_ref, grad_hbm, pgrad_hbm,
    grad_ref, bar_ref, pgrad_ref, layer_sem, sem,
):
    layers, rows, cols = g_ref.shape[1:]
    bricks = layers * rows

    def first_back(z, r):
        v = [v_ref[i, z, r, :] for i in range(3)]
        m = [m_ref[i, z, r, :] for i in range(3)]
        back, bar = collide_back([g_ref[q, z, r, :] for q in range(Q)], m, v, s_ref[z, r, :])
        bar_ref[z, r, :] = sb_ref[z, r, :] + bar
        for q, value in enumerate(back):
            grad_ref[q, z, r, :] = value

    stores = [
        pltpu.make_async_copy(grad_ref.at[:, z], grad_hbm.at[:, z], layer_sem.at[z]) for z in range(layers)
    ]
    for z in range(layers):
        each_chunk(1, rows, 16, first_back, z)
        stores[z].start()

    ids = ids_ref[0]
    slots = slot_ref[0]
    listed = ids.shape[1]
    hit = lax.broadcasted_iota(jnp.int32, (bricks, listed), 0) == ids
    sums = jnp.sum(bar_ref[...].reshape(bricks, cols), axis=1, keepdims=True)
    brick_sum = jnp.sum(jnp.where(hit, sums, 0.0), axis=0, keepdims=True)
    table = pgrad_ref.shape[2]
    slot_of_row = lax.broadcasted_iota(jnp.int32, (table, listed), 0)
    slot_sum = jnp.sum(jnp.where(slot_of_row == slots, brick_sum, 0.0), axis=1, keepdims=True)
    diagonal = lax.broadcasted_iota(jnp.int32, (table, table), 0) == lax.broadcasted_iota(
        jnp.int32, (table, table), 1
    )
    pgrad_ref[0] = jnp.sum(jnp.where(diagonal, slot_sum, 0.0), axis=0, keepdims=True)
    last = pltpu.make_async_copy(pgrad_ref, pgrad_hbm, sem)
    last.start()
    for copy in stores + [last]:
        copy.wait()


def on_device(f_start, cotangent, porosity, brick_ids, brick_slot):
    _, layers, rows, cols = f_start.shape
    vmem = pl.BlockSpec(memory_space=pltpu.VMEM)
    hbm = pl.BlockSpec(memory_space=pltpu.HBM)
    field = pltpu.VMEM((Q, layers, rows, cols), jnp.float32)

    def up8(count):
        return -(-count // 8) * 8

    halos = []
    for kinds in (2, 1):
        x = pltpu.VMEM((2, rows, cols), jnp.float32)
        y = pltpu.VMEM((2, up8(kinds * 5 * layers), cols), jnp.float32)
        c = pltpu.VMEM((4, up8(kinds * layers), cols), jnp.float32)
        halos += [x, x, y, y, c, c]

    def array(*shape):
        return jax.ShapeDtypeStruct(shape, jnp.float32)

    operands = [
        pltpu.with_memory_space_constraint(operand, pltpu.HBM)
        for operand in (f_start, cotangent, porosity, brick_ids, brick_slot)
    ]
    held = pl.pallas_call(
        forward_kernel,
        out_shape=(
            array(Q, layers, rows, cols),
            array(layers, rows, cols),
            array(3, layers, rows, cols),
            array(3, layers, rows, cols),
            array(layers, rows, cols),
            jax.ShapeDtypeStruct(brick_ids.shape, brick_ids.dtype),
            jax.ShapeDtypeStruct(brick_slot.shape, brick_slot.dtype),
        ),
        in_specs=[hbm] * 5,
        out_specs=(vmem,) * 7,
        scratch_shapes=[
            field,
            pltpu.VMEM(cotangent.shape, cotangent.dtype),
            pltpu.SMEM(porosity.shape, porosity.dtype),
            field,
            field,
        ]
        + halos
        + [
            pltpu.SemaphoreType.DMA((4,)),
            pltpu.SemaphoreType.DMA((layers,)),
            pltpu.SemaphoreType.DMA((2, 8)),
            pltpu.SemaphoreType.DMA((2, 8)),
        ],
        compiler_params=pltpu.CompilerParams(
            collective_id=0, has_side_effects=True, vmem_limit_bytes=24 * 1024 * 1024
        ),
    )(*operands)
    return pl.pallas_call(
        last_kernel,
        out_shape=(array(*f_start.shape), array(*porosity.shape)),
        in_specs=[vmem] * 7,
        out_specs=(hbm, hbm),
        scratch_shapes=[
            field,
            pltpu.VMEM((layers, rows, cols), jnp.float32),
            pltpu.VMEM(porosity.shape, jnp.float32),
            pltpu.SemaphoreType.DMA((layers,)),
            pltpu.SemaphoreType.DMA,
        ],
        compiler_params=pltpu.CompilerParams(vmem_limit_bytes=24 * 1024 * 1024),
    )(*held)


def solution(mesh):
    field = P(None, None, "gy", "gx")
    table = P("gx", "gy", None)
    return jax.shard_map(
        on_device,
        mesh=mesh,
        in_specs=(field, field, table, table, table),
        out_specs=(field, table),
        check_vma=False,
    )
```

```python
import jax
import jax.numpy as jnp
from jax import lax
from jax.experimental import pallas as pl
from jax.experimental.pallas import tpu as pltpu
from jax.sharding import PartitionSpec as P

EX = (0, 1, -1, 0, 0, 0, 0, 1, -1, 1, -1, 1, -1, 1, -1, 0, 0, 0, 0)
EY = (0, 0, 0, 1, -1, 0, 0, 1, 1, -1, -1, 0, 0, 0, 0, 1, -1, 1, -1)
EZ = (0, 0, 0, 0, 0, 1, -1, 0, 0, 0, 0, 1, 1, -1, -1, 1, 1, -1, -1)
Q = 19
PAIRS = ((1, 2), (3, 4), (5, 6), (7, 10), (9, 8), (11, 14), (13, 12), (15, 18), (17, 16))
AXIS_W = 1.0 / 18.0
EDGE_W = 1.0 / 36.0
MESH = pl.DeviceIdType.MESH


def rank_among(q, component):
    return [p for p in range(Q) if component[p] == component[q]].index(q)


def side(step):
    return 0 if step > 0 else 1


def moments(d):
    return (
        (d[0], d[3] + d[4] + d[5] + d[6]),
        (d[1], (d[3] - d[4]) + (d[7] + d[8])),
        (d[2], (d[5] - d[6]) + (d[7] - d[8])),
    )


def along(vec):
    x, y, z = vec
    return (x, y, z, x + y, x - y, x + z, x - z, y + z, y - z)


def density_velocity(f, s):
    rho = f[0]
    diffs = []
    for a, b in PAIRS:
        rho = rho + (f[a] + f[b])
        diffs.append(f[a] - f[b])
    m = [a + b for a, b in moments(diffs)]
    inverse = s / rho
    return rho, m, [c * inverse for c in m]


def collide(f, rho, v):
    square = v[0] * v[0] + v[1] * v[1] + v[2] * v[2]
    base = 1.0 - 1.5 * square
    out = [None] * Q
    rho_axis = (0.8 * AXIS_W) * rho
    rho_edge = (0.8 * EDGE_W) * rho
    out[0] = 0.2 * f[0] + (0.8 / 3.0) * rho * base
    for n, ((a, b), c) in enumerate(zip(PAIRS, along(v))):
        scale = rho_axis if n < 3 else rho_edge
        even = scale * (base + 4.5 * c * c)
        odd = scale * (3.0 * c)
        out[a] = 0.2 * f[a] + (even + odd)
        out[b] = 0.2 * f[b] + (even - odd)
    return out


def collide_back(g, m, v, s):
    p = [g[a] + g[b] for a, b in PAIRS]
    d = [g[a] - g[b] for a, b in PAIRS]
    g1 = [AXIS_W * a + EDGE_W * b for a, b in moments(d)]
    xy, xz, yz = p[3] + p[4], p[5] + p[6], p[7] + p[8]
    g0 = (1.0 / 3.0) * g[0] + AXIS_W * (p[0] + p[1] + p[2]) + EDGE_W * (xy + xz + yz)
    gxx = AXIS_W * p[0] + EDGE_W * (xy + xz)
    gyy = AXIS_W * p[1] + EDGE_W * (xy + yz)
    gzz = AXIS_W * p[2] + EDGE_W * (xz + yz)
    gxy = EDGE_W * (p[3] - p[4])
    gxz = EDGE_W * (p[5] - p[6])
    gyz = EDGE_W * (p[7] - p[8])
    h = (
        gxx * v[0] + gxy * v[1] + gxz * v[2],
        gxy * v[0] + gyy * v[1] + gyz * v[2],
        gxz * v[0] + gyz * v[1] + gzz * v[2],
    )
    square = v[0] * v[0] + v[1] * v[1] + v[2] * v[2]
    b = [3.0 * g1[i] + 9.0 * h[i] - 3.0 * (g0 * v[i]) for i in range(3)]
    rest = g0 * (1.0 + 1.5 * square) - 4.5 * (v[0] * h[0] + v[1] * h[1] + v[2] * h[2])
    base = 0.8 * rest
    scale = 0.8 * s
    out = [None] * Q
    out[0] = 0.2 * g[0] + base
    for (a, o), c in zip(PAIRS, along([scale * c for c in b])):
        out[a] = 0.2 * g[a] + (base + c)
        out[o] = 0.2 * g[o] + (base - c)
    solid_bar = -0.8 * (b[0] * m[0] + b[1] * m[1] + b[2] * m[2])
    return out, solid_bar


def each_chunk(layers, rows, step_rows, body, first=0):
    chunks = rows // step_rows

    def step(i, carry):
        body(first + lax.div(i, chunks), pl.ds(pl.multiple_of(lax.rem(i, chunks) * step_rows, step_rows), step_rows))
        return carry

    lax.fori_loop(0, layers * chunks, step, 0)


def forward_kernel(
    f_hbm, cot_hbm, por_hbm, ids_hbm, slot_hbm,
    a_ref, s_ref, v_ref, m_ref, sb_ref, ids_ref, slot_ref,
    f_ref, cot_ref, por_ref, b_ref, c_ref,
    xs1, xr1, ys1, yr1, cs1, cr1, xs2, xr2, ys2, yr2, cs2, cr2, load_sem, layer_sem, send_sem, recv_sem,
):
    layers, rows, cols = f_ref.shape[1:]
    n_x, n_y = lax.axis_size("gx"), lax.axis_size("gy")
    my_x, my_y = lax.axis_index("gx"), lax.axis_index("gy")

    def device(dx, dy):
        return (lax.rem(my_x + dx + n_x, n_x), lax.rem(my_y + dy + n_y, n_y))

    straight = ((1, 0), (-1, 0), (0, 1), (0, -1))
    corners = ((1, 1), (1, -1), (-1, 1), (-1, -1))
    barrier = pltpu.get_barrier_semaphore()
    loads = [
        pltpu.make_async_copy(src, dst, load_sem.at[n])
        for n, (src, dst) in enumerate(
            ((por_hbm, por_ref), (ids_hbm, ids_ref), (slot_hbm, slot_ref), (cot_hbm, cot_ref))
        )
    ]
    layer_loads = [
        pltpu.make_async_copy(f_hbm.at[:, z], f_ref.at[:, z], layer_sem.at[z]) for z in range(layers)
    ]
    for copy in loads + layer_loads:
        copy.start()
    for dx, dy in straight + corners:
        pl.semaphore_signal(barrier, inc=1, device_id=device(dx, dy), device_id_type=MESH)

    lane = lax.broadcasted_iota(jnp.int32, (rows, cols), 1)
    lane1 = lax.broadcasted_iota(jnp.int32, (1, cols), 1)

    def copies(phase, xs, xr, ys, yr, cs, cr):
        out = []
        for n, (dx, dy) in enumerate(straight + corners):
            if n < 2:
                src, dst = xs.at[n], xr.at[n]
            elif n < 4:
                src, dst = ys.at[n - 2], yr.at[n - 2]
            else:
                src, dst = cs.at[n - 4], cr.at[n - 4]
            out.append(
                pltpu.make_async_remote_copy(
                    src_ref=src, dst_ref=dst,
                    send_sem=send_sem.at[phase, n], recv_sem=recv_sem.at[phase, n],
                    device_id=device(dx, dy), device_id_type=MESH,
                )
            )
        return out[4:] + out[:4]

    def pack(read, sign, kind, ys, cs, carry):
        def layer(z, carry):
            carry = list(carry)
            for q in range(Q):
                dx, dy = sign * EX[q], sign * EY[q]
                if not dx and not dy:
                    continue
                plane = read(q, z)
                if dx:
                    j = kind * 5 * layers + rank_among(q, EX) * layers + z
                    start = cols - 1 if dx > 0 else 0
                    moved = pltpu.roll(plane, lax.rem(j - start + cols, cols), 1)
                    carry[side(dx)] = jnp.where(lane == j, moved, carry[side(dx)])
                if dy:
                    jy = kind * 5 * layers + rank_among(q, EY) * layers + z
                    edge = plane[rows - 8 :] if dy > 0 else plane[:8]
                    if dx:
                        edge = pltpu.roll(edge, dx % cols, 1)
                    edge = edge[7:8] if dy > 0 else edge[0:1]
                    ys[side(dy), pl.ds(jy, 1), :] = edge
                    if dx:
                        cs[2 * side(dx) + side(dy), pl.ds(kind * layers + z, 1), :] = edge
            return tuple(carry)

        return lax.fori_loop(0, layers, layer, carry, unroll=True)

    def stream(read, sign, out):
        def layer(z, carry):
            for q in range(Q):
                dx, dy, dz = sign * EX[q], sign * EY[q], sign * EZ[q]
                plane = read(q, lax.rem(z - dz + layers, layers) if dz else z)
                if dx:
                    plane = pltpu.roll(plane, dx % cols, 1)
                if dy:
                    plane = pltpu.roll(plane, dy % rows, 0)
                out[q, z] = plane
            return carry

        lax.fori_loop(0, layers, layer, 0, unroll=True)

    def edges(sign, kind, xr, yr, cr, out):
        def layer(z, carry):
            planes, lines = [], []
            for q in range(Q):
                dx, dy, dz = sign * EX[q], sign * EY[q], sign * EZ[q]
                from_z = lax.rem(z - dz + layers, layers) if dz else z
                end = 0 if dx > 0 else cols - 1
                if dx:
                    j = kind * 5 * layers + rank_among(q, EX) * layers + from_z
                    column = pltpu.roll(xr[side(dx)], lax.rem(end - j + cols, cols), 1)
                    if dy:
                        column = pltpu.roll(column, dy % rows, 0)
                    planes.append((q, jnp.where(lane == end, column, out[q, z])))
                if dy:
                    jy = kind * 5 * layers + rank_among(q, EY) * layers + from_z
                    line = yr[side(dy), pl.ds(jy, 1), :]
                    if dx:
                        corner = cr[2 * side(dx) + side(dy), pl.ds(kind * layers + from_z, 1), :]
                        line = jnp.where(lane1 == end, corner, line)
                    lines.append((q, 0 if dy > 0 else rows - 1, line))
            for q, plane in planes:
                out[q, z] = plane
            for q, at, line in lines:
                out[q, z, at : at + 1, :] = line
            return carry

        lax.fori_loop(0, layers, layer, 0, unroll=True)

    for copy in loads[:3]:
        copy.wait()
    bricks = layers * rows
    ids = ids_ref[0]
    slots = slot_ref[0]
    listed = ids.shape[1]
    value = jnp.zeros((1, listed), jnp.float32)
    for k in range(por_ref.shape[2]):
        value = jnp.where(slots == k, por_ref[0, 0, k], value)
    hit = lax.broadcasted_iota(jnp.int32, (bricks, listed), 0) == ids
    solid = jnp.sum(jnp.where(hit, value, 0.0), axis=1, keepdims=True)
    s_ref[...] = jnp.broadcast_to(1.0 - solid, (bricks, cols)).reshape(layers, rows, cols)

    def read_c(q, z):
        return c_ref[q, z]

    def read_cot(q, z):
        return cot_ref[q, z].astype(jnp.float32)

    zero = jnp.zeros((rows, cols), jnp.float32)
    loads[3].wait()
    ends = pack(read_cot, -1, 1, ys1, cs1, (zero, zero))

    def first_collision(z, r):
        f = [f_ref[q, z, r, :] for q in range(Q)]
        rho, m, v = density_velocity(f, s_ref[z, r, :])
        for i in range(3):
            v_ref[i, z, r, :] = v[i]
            m_ref[i, z, r, :] = m[i]
        for q, value in enumerate(collide(f, rho, v)):
            c_ref[q, z, r, :] = value

    for z in range(layers):
        layer_loads[z].wait()
        each_chunk(1, rows, 16, first_collision, z)

    ends = pack(read_c, 1, 0, ys1, cs1, ends)
    xs1[0] = ends[0]
    xs1[1] = ends[1]
    pl.semaphore_wait(barrier, len(straight + corners))
    first = copies(0, xs1, xr1, ys1, yr1, cs1, cr1)
    for copy in first:
        copy.start()
    stream(read_c, 1, a_ref)
    stream(read_cot, -1, b_ref)
    for copy in first:
        copy.wait()
    edges(1, 0, xr1, yr1, cr1, a_ref)
    edges(-1, 1, xr1, yr1, cr1, b_ref)

    def second_back(z, r):
        s = s_ref[z, r, :]
        rho, m, v = density_velocity([a_ref[q, z, r, :] for q in range(Q)], s)
        back, bar = collide_back([b_ref[q, z, r, :] for q in range(Q)], m, v, s)
        sb_ref[z, r, :] = bar
        for q, value in enumerate(back):
            c_ref[q, z, r, :] = value

    each_chunk(layers, rows, 16, second_back)

    ends = pack(read_c, -1, 0, ys2, cs2, (zero, zero))
    xs2[0] = ends[0]
    xs2[1] = ends[1]
    second = copies(1, xs2, xr2, ys2, yr2, cs2, cr2)
    for copy in second:
        copy.start()
    stream(read_c, -1, a_ref)
    for copy in second:
        copy.wait()
    edges(-1, 0, xr2, yr2, cr2, a_ref)


def last_kernel(
    g_ref, s_ref, v_ref, m_ref, sb_ref, ids_ref, slot_ref, grad_hbm, pgrad_hbm,
    grad_ref, bar_ref, pgrad_ref, layer_sem, sem,
):
    layers, rows, cols = g_ref.shape[1:]
    bricks = layers * rows

    def first_back(z, r):
        v = [v_ref[i, z, r, :] for i in range(3)]
        m = [m_ref[i, z, r, :] for i in range(3)]
        back, bar = collide_back([g_ref[q, z, r, :] for q in range(Q)], m, v, s_ref[z, r, :])
        bar_ref[z, r, :] = sb_ref[z, r, :] + bar
        for q, value in enumerate(back):
            grad_ref[q, z, r, :] = value

    stores = [
        pltpu.make_async_copy(grad_ref.at[:, z], grad_hbm.at[:, z], layer_sem.at[z]) for z in range(layers)
    ]
    for z in range(layers):
        each_chunk(1, rows, 16, first_back, z)
        stores[z].start()

    ids = ids_ref[0]
    slots = slot_ref[0]
    listed = ids.shape[1]
    hit = lax.broadcasted_iota(jnp.int32, (bricks, listed), 0) == ids
    sums = jnp.sum(bar_ref[...].reshape(bricks, cols), axis=1, keepdims=True)
    brick_sum = jnp.sum(jnp.where(hit, sums, 0.0), axis=0, keepdims=True)
    table = pgrad_ref.shape[2]
    slot_of_row = lax.broadcasted_iota(jnp.int32, (table, listed), 0)
    slot_sum = jnp.sum(jnp.where(slot_of_row == slots, brick_sum, 0.0), axis=1, keepdims=True)
    diagonal = lax.broadcasted_iota(jnp.int32, (table, table), 0) == lax.broadcasted_iota(
        jnp.int32, (table, table), 1
    )
    pgrad_ref[0] = jnp.sum(jnp.where(diagonal, slot_sum, 0.0), axis=0, keepdims=True)
    last = pltpu.make_async_copy(pgrad_ref, pgrad_hbm, sem)
    last.start()
    for copy in stores + [last]:
        copy.wait()


def on_device(f_start, cotangent, porosity, brick_ids, brick_slot):
    _, layers, rows, cols = f_start.shape
    vmem = pl.BlockSpec(memory_space=pltpu.VMEM)
    hbm = pl.BlockSpec(memory_space=pltpu.HBM)
    field = pltpu.VMEM((Q, layers, rows, cols), jnp.float32)

    def up8(count):
        return -(-count // 8) * 8

    halos = []
    for kinds in (2, 1):
        x = pltpu.VMEM((2, rows, cols), jnp.float32)
        y = pltpu.VMEM((2, up8(kinds * 5 * layers), cols), jnp.float32)
        c = pltpu.VMEM((4, up8(kinds * layers), cols), jnp.float32)
        halos += [x, x, y, y, c, c]

    def array(*shape):
        return jax.ShapeDtypeStruct(shape, jnp.float32)

    operands = [
        pltpu.with_memory_space_constraint(operand, pltpu.HBM)
        for operand in (f_start, cotangent, porosity, brick_ids, brick_slot)
    ]
    held = pl.pallas_call(
        forward_kernel,
        out_shape=(
            array(Q, layers, rows, cols),
            array(layers, rows, cols),
            array(3, layers, rows, cols),
            array(3, layers, rows, cols),
            array(layers, rows, cols),
            jax.ShapeDtypeStruct(brick_ids.shape, brick_ids.dtype),
            jax.ShapeDtypeStruct(brick_slot.shape, brick_slot.dtype),
        ),
        in_specs=[hbm] * 5,
        out_specs=(vmem,) * 7,
        scratch_shapes=[
            field,
            pltpu.VMEM(cotangent.shape, cotangent.dtype),
            pltpu.SMEM(porosity.shape, porosity.dtype),
            field,
            field,
        ]
        + halos
        + [
            pltpu.SemaphoreType.DMA((4,)),
            pltpu.SemaphoreType.DMA((layers,)),
            pltpu.SemaphoreType.DMA((2, 8)),
            pltpu.SemaphoreType.DMA((2, 8)),
        ],
        compiler_params=pltpu.CompilerParams(
            collective_id=0, has_side_effects=True, vmem_limit_bytes=24 * 1024 * 1024
        ),
    )(*operands)
    return pl.pallas_call(
        last_kernel,
        out_shape=(array(*f_start.shape), array(*porosity.shape)),
        in_specs=[vmem] * 7,
        out_specs=(hbm, hbm),
        scratch_shapes=[
            field,
            pltpu.VMEM((layers, rows, cols), jnp.float32),
            pltpu.VMEM(porosity.shape, jnp.float32),
            pltpu.SemaphoreType.DMA((layers,)),
            pltpu.SemaphoreType.DMA,
        ],
        compiler_params=pltpu.CompilerParams(vmem_limit_bytes=24 * 1024 * 1024),
    )(*held)


def solution(mesh):
    field = P(None, None, "gy", "gx")
    table = P("gx", "gy", None)
    return jax.shard_map(
        on_device,
        mesh=mesh,
        in_specs=(field, field, table, table, table),
        out_specs=(field, table),
        check_vma=False,
    )
```
